256 devices in a mesh: fsdp: 64 (over x, z, core), rep: 4 (over y).
Axes of the slice: x: 4, y: 4, z: 8, core: 2. Of those that a mesh axis runs over, the one named last changes fastest.
Arguments:
- grad: float32 [4, 256, 65536], P('rep', 'fsdp'), may hold values from -45 to 45
- z_params: float32 [4, 256, 65536], P('rep', 'fsdp'), may hold values from -6 to 6
- x_params: float32 [4, 256, 65536], P('rep', 'fsdp'), may hold values from -6 to 6
- owner: int32 [64], replicated, may hold values from 0 to 63, each once
- stat_left: float32 [64, 1024, 1024], P('fsdp', 'rep'), may hold values from -6 to 6
- stat_right: float32 [64, 1024, 1024], P('fsdp', 'rep'), may hold values from -6 to 6
- root_left: bfloat16 [64, 1024, 1024], P('fsdp', 'rep'), may hold values from -0.1875 to 0.1875
- root_right: bfloat16 [64, 1024, 1024], P('fsdp', 'rep'), may hold values from -0.1875 to 0.1875
Outputs:
- z_new: float32 [4, 256, 65536], P('rep', 'fsdp')
- x_new: float32 [4, 256, 65536], P('rep', 'fsdp')
- y_new: bfloat16 [4, 256, 65536], P('rep', 'fsdp')
- left_new: float32 [64, 1024, 1024], P('fsdp', 'rep')
- right_new: float32 [64, 1024, 1024], P('fsdp', 'rep')
The draws below stay inside these ranges and needn't reach their ends.
Inputs may be any that keep to these rules, and one draw needn't show every extreme that they name: `owner`: each fsdp index owns exactly one block.
All inputs are finite; a program needn't handle non-finite values.
Results may differ from the reference program's by a relative error of at most 0.0025.
Values may be sent and summed in bfloat16 or wider, within the bound.
A program may use at most 320 MiB of HBM per device.

```python
import math
import jax
import jax.numpy as jnp
from jax import lax

BLK = 1024
NB = 64
COLS = 65536
Q = 256
N_REP = 4


def draw_grad(key, part):
    key = jax.random.fold_in(key, 11)
    key_base, key_rows, key_cols = jax.random.split(key, 3)
    shape = (N_REP, Q, COLS)
    base = jnp.clip(jax.random.normal(key_base, shape, jnp.float32), -5.0, 5.0)
    lower, upper = (0.3, 3.0)
    row_scale = jnp.exp(jax.random.uniform(key_rows, (N_REP, Q, 1), jnp.float32, math.log(lower), math.log(upper)))
    col_scale = jnp.exp(jax.random.uniform(key_cols, (1, 1, COLS), jnp.float32, math.log(lower), math.log(upper)))
    return (base * row_scale * col_scale).astype(jnp.float32)


def levels(stream_key, extent, shards, least, top_value):
    level = 1.0
    for dim, shards_of in shards:
        heights = jax.random.uniform(jax.random.fold_in(jax.random.fold_in(stream_key, 6), dim), (shards_of,), jnp.float32, least / len(shards), top_value / len(shards))
        level = level * jnp.repeat(jnp.exp(heights), extent[dim] // shards_of).reshape((-1,) + (1,) * (len(extent) - 1 - dim))
    return level


def centred(stream_key, extent, width, limit, cuts=(), held_as=jnp.bfloat16):
    drawn = jax.random.normal(stream_key, extent, jnp.float32) * width
    if len(cuts) > 0:
        drawn = levels(stream_key, extent, cuts, -0.22, 0.18) * drawn
    return jnp.clip(drawn, min=-limit, max=limit).astype(held_as)


def setup_inputs(seed: int = 0) -> dict:
    key_of = jax.random.split(jax.random.key(seed), 9)
    grad = draw_grad(jax.random.fold_in(key_of[8], 71), 0)
    z_params = centred(key_of[1], (N_REP, Q, COLS), 1.0, 6.0, ((0, 4), (1, 64)), jnp.float32)
    x_params = centred(key_of[2], (N_REP, Q, COLS), 1.0, 6.0, ((0, 4), (1, 64)), jnp.float32)
    owner = jax.random.permutation(key_of[3], NB).astype(jnp.int32)
    stat_left = centred(key_of[4], (NB, BLK, BLK), 1.0, 6.0, ((0, 64), (1, 4)), jnp.float32)
    stat_right = centred(key_of[5], (NB, BLK, BLK), 1.0, 6.0, ((0, 64), (1, 4)), jnp.float32)
    root_left = centred(key_of[6], (NB, BLK, BLK), BLK ** -0.5, 0.1875, ((0, 64), (1, 4)))
    root_right = centred(key_of[7], (NB, BLK, BLK), BLK ** -0.5, 0.1875, ((0, 64), (1, 4)))
    return {"grad": grad, "z_params": z_params, "x_params": x_params, "owner": owner, "stat_left": stat_left, "stat_right": stat_right, "root_left": root_left, "root_right": root_right}


def reference(grad, z_params, x_params, owner, stat_left, stat_right, root_left, root_right):
    whole = grad.reshape(BLK, COLS)
    inverse = jnp.argsort(owner).astype(jnp.int32)
    count = owner.shape[0]

    def one_block(slot):
        block_id = inverse[slot]
        block = lax.dynamic_slice_in_dim(whole, block_id * BLK, BLK, 1)
        left = 0.95 * stat_left[slot] + 0.05 / BLK * jnp.dot(block, block.T, precision=lax.Precision.HIGHEST)
        right = 0.95 * stat_right[slot] + 0.05 / BLK * jnp.dot(block.T, block, precision=lax.Precision.HIGHEST)
        left_prod = jnp.dot(root_left[slot], block.astype(jnp.bfloat16), preferred_element_type=jnp.float32).astype(jnp.bfloat16)
        precond = jnp.dot(left_prod, root_right[slot], preferred_element_type=jnp.float32)
        scale = jnp.sqrt(jnp.mean(block * block)) * lax.rsqrt(jnp.mean(precond * precond) + 1e-06)
        return (left, right, (scale * precond).astype(jnp.bfloat16))
    left_new, right_new, directions = lax.map(one_block, jnp.arange(count, dtype=jnp.int32))
    ordered = directions[owner]
    flat_dir = jnp.transpose(ordered, (1, 0, 2)).reshape(grad.shape)
    z_new = z_params - 0.2 * flat_dir.astype(jnp.float32)
    x_new = 0.75 * x_params + 0.25 * z_new
    y_new = (0.1 * z_new + 0.9 * x_new).astype(jnp.bfloat16)
    return (z_new, x_new, y_new, left_new, right_new)
```

```python
import functools

import jax
import jax.numpy as jnp
from jax import lax
from jax.experimental import pallas as pl
from jax.experimental.pallas import tpu as pltpu
from jax.sharding import PartitionSpec as P

MESH = pl.DeviceIdType.MESH
F32 = jnp.float32
BF16 = jnp.bfloat16

NB = 64
BLK = 1024
Q = 256
LINE = 16
CH = 4


def iota(shape, dim):
    return lax.broadcasted_iota(jnp.int32, shape, dim)


def fold(v):
    rows, cols = v.shape
    total = v[:, 0:128]
    for j in range(1, cols // 128):
        total = total + v[:, 128 * j : 128 * (j + 1)]
    return jnp.sum(total.reshape(rows // 8, 8, 128), axis=0)


def remote_kernel(
    inv_ref, own_ref, grad_ref, z_ref, x_ref, sl_ref, sr_ref, rl_ref, rr_ref,
    z_o, x_o, y_o, l_o, r_o,
    gbuf, send, held, gq, bc, ac, lg, lgb, zbuf, xbuf, slbuf, srbuf,
    perm1, perm2, dsend, dret, part, scl, sclsend,
    loc, line_sem, y_s1, y_s2, y_r1, y_r2, g_s, g_r, d_s, d_r, p_s, p_r, s_s, s_r,
):
    f = lax.axis_index("fsdp")
    r = lax.axis_index("rep")
    fx, fz, fc = f // LINE, (f % LINE) // 2, f % 2
    right, left, across = (r + 1) % 4, (r + 3) % 4, (r + 2) % 4

    def peer(j, i):
        return ((fx + j) % 4) * LINE + ((fz + i // 2) % 8) * 2 + (fc + i) % 2

    barrier = pltpu.get_barrier_semaphore()

    def greet(i, c):
        pl.semaphore_signal(barrier, inc=1, device_id={"fsdp": peer(0, i)}, device_id_type=MESH)
        return c

    lax.fori_loop(1, LINE, greet, 0)
    for d in (1, 2, 3):
        pl.semaphore_signal(barrier, inc=1, device_id={"fsdp": peer(d, 0)}, device_id_type=MESH)
        pl.semaphore_signal(barrier, inc=1, device_id={"rep": (r + d) % 4}, device_id_type=MESH)

    loads = [pltpu.make_async_copy(grad_ref, gbuf, loc.at[0])]
    for c in range(CH):
        loads.append(
            pltpu.make_async_copy(rr_ref.at[:, pl.ds(Q * c, Q)], bc.at[c, r], loc.at[1 + c])
        )
    for c in range(4):
        loads.append(
            pltpu.make_async_copy(rl_ref.at[:, pl.ds(Q * c, Q)], ac.at[c], loc.at[5 + c])
        )
    for n, (a, b) in enumerate(((sl_ref, slbuf), (sr_ref, srbuf), (z_ref, zbuf), (x_ref, xbuf))):
        loads.append(pltpu.make_async_copy(a, b, loc.at[9 + n]))
    for load in loads:
        load.start()

    o, i = iota((Q, Q), 0), iota((Q, Q), 1)
    perm1[...] = (((i % 32) // 4) * 32 + (i // 32) * 4 + i % 4 == o).astype(F32).astype(BF16)
    perm2[...] = (((i % 128) // 4) * 8 + (i // 128) * 4 + i % 4 == o).astype(F32).astype(BF16)

    loads[0].wait()

    def prepare(s, c):
        send[s] = gbuf[inv_ref[s]].astype(BF16)
        return c

    lax.fori_loop(0, NB, prepare, 0, unroll=4)
    held[f] = send[f]
    for c in range(CH):
        loads[1 + c].wait()

    def ring(n, ref, sub, half0, half1):
        def first():
            for side, to in ((0, right), (1, left)):
                pltpu.make_async_remote_copy(
                    sub(ref, r), sub(ref, r), y_s1.at[n, side], y_r1.at[n, side],
                    device_id={"rep": to}, device_id_type=MESH,
                ).start()

        def second():
            for side, to, frm, half in ((0, right, left, half0), (1, left, right, half1)):
                pltpu.make_async_remote_copy(
                    sub(ref, frm), sub(ref, frm), y_s1.at[n, side], y_r1.at[n, side],
                    device_id={"rep": to}, device_id_type=MESH,
                ).wait_recv()
                pltpu.make_async_remote_copy(
                    half(ref, frm), half(ref, frm), y_s2.at[n, side], y_r2.at[n, side],
                    device_id={"rep": to}, device_id_type=MESH,
                ).start()

        def done():
            for side, to, half in ((0, right, half0), (1, left, half1)):
                pltpu.make_async_remote_copy(
                    half(ref, across), half(ref, across), y_s2.at[n, side], y_r2.at[n, side],
                    device_id={"rep": to}, device_id_type=MESH,
                ).wait_recv()

        def drain():
            for side, to, half in ((0, right, half0), (1, left, half1)):
                pltpu.make_async_remote_copy(
                    sub(ref, r), sub(ref, r), y_s1.at[n, side], y_r1.at[n, side],
                    device_id={"rep": to}, device_id_type=MESH,
                ).wait_send()
                pltpu.make_async_remote_copy(
                    half(ref, r), half(ref, r), y_s2.at[n, side], y_r2.at[n, side],
                    device_id={"rep": to}, device_id_type=MESH,
                ).wait_send()

        return first, second, done, drain

    def rows_of(start, size):
        return lambda ref, k: ref.at[k, pl.ds(start, size)]

    b_ring = [
        ring(c, bc.at[c], rows_of(0, Q), rows_of(0, Q // 2), rows_of(Q // 2, Q // 2))
        for c in range(CH)
    ]
    g_ring = []
    for j in range(4):
        base = pl.multiple_of(((fx + 4 - j) % 4) * 64, 64)
        g_ring.append(
            ring(4 + j, gq, rows_of(base, 64), rows_of(base, 32), rows_of(base + 32, 32))
        )

    def g_copy(j, i):
        to = peer(j, i)
        return pltpu.make_async_remote_copy(
            send.at[to], held.at[f], g_s.at[0], g_r.at[j],
            device_id={"fsdp": to}, device_id_type=MESH,
        )

    def g_send(j):
        def body(i, c):
            g_copy(j, i).start()
            return c

        lax.fori_loop(1 if j == 0 else 0, LINE, body, 0)

    def g_take(j):
        count = 15 if j == 0 else 16
        pltpu.make_async_remote_copy(
            send.at[pl.ds(0, count)], held.at[pl.ds(0, count)], g_s.at[0], g_r.at[j],
            device_id={"fsdp": peer(1, 0)}, device_id_type=MESH,
        ).wait_recv()
        line = (fx + 4 - j) % 4
        pieces = jnp.concatenate(
            [held[pl.ds(line * LINE + 8 * h, 8)].reshape(Q, 128) for h in range(2)], axis=1
        )
        rows = jnp.dot(perm1[...], pieces, preferred_element_type=F32).astype(BF16)
        for h in range(2):
            at = pl.multiple_of(line * 64 + 32 * h, 32)
            for t in range(8):
                gq[r, pl.ds(at, 32), 128 * t : 128 * (t + 1)] = rows[
                    32 * t : 32 * (t + 1), 128 * h : 128 * (h + 1)
                ]

    pl.semaphore_wait(barrier, 21)
    for d in (1, 2, 3):
        pl.semaphore_signal(line_sem, inc=1, device_id={"fsdp": peer(d, 0)}, device_id_type=MESH)
    g_send(0)
    b_ring[0][0]()
    b_ring[1][0]()
    pl.semaphore_wait(line_sem, 3)
    for j in range(1, 4):
        g_send(j)

    for load in loads[5:]:
        load.wait()

    def left_root(k, first):
        gk = gq.at[k]
        for n in range(4):
            cols = slice(Q * n, Q * (n + 1))
            term = jnp.dot(ac[k], gk[:, cols], preferred_element_type=F32)
            lg[:, cols] = term if first else lg[:, cols] + term

    def stats(k, first):
        gk = gq.at[k]
        l_o[:, pl.ds(pl.multiple_of(k * Q, Q), Q)] = lax.dot_general(
            gq[r], gk[...], (((1,), (1,)), ((), ())), preferred_element_type=F32
        )
        strip = gk[:, pl.ds(pl.multiple_of(r * Q, Q), Q)]
        for n in range(4):
            cols = slice(Q * n, Q * (n + 1))
            term = lax.dot_general(
                strip, gk[:, cols], (((0,), (0,)), ((), ())), preferred_element_type=F32
            )
            r_o[:, cols] = term if first else r_o[:, cols] + term

    b_ring[0][1]()
    g_take(0)
    g_ring[0][0]()
    b_ring[1][1]()
    g_take(1)
    g_ring[1][0]()
    g_ring[0][1]()
    g_take(2)
    g_ring[2][0]()
    g_ring[1][1]()
    g_take(3)
    g_ring[3][0]()
    b_ring[2][0]()
    own = gq[r].astype(F32)
    part[r, 1] = fold(own * own)
    left_root(r, True)
    stats(r, True)
    g_ring[2][1]()
    g_ring[3][1]()
    b_ring[3][0]()
    left_root(left, False)
    left_root(right, False)
    b_ring[2][1]()
    stats(left, False)
    for n in range(4):
        g_ring[n][2]()
    left_root(across, False)
    lgb[...] = lg[...].astype(BF16)

    def d_send(c):
        def body(i, carry):
            to = peer(i // LINE, i % LINE)
            pltpu.make_async_remote_copy(
                dsend.at[c, to], dret.at[c, f], d_s.at[c], d_r.at[c],
                device_id={"fsdp": to}, device_id_type=MESH,
            ).start()
            return carry

        lax.fori_loop(1, NB, body, 0)
        dret[c, f] = dsend[c, f]

    def product(c):
        b_ring[c][2]()
        p = jnp.dot(lgb[...], bc[c].reshape(BLK, Q), preferred_element_type=F32)
        squares = fold(p * p)
        part[r, 0] = squares if c == 0 else part[r, 0] + squares
        pb = p.astype(BF16)
        for h in range(2):
            rows = slice(128 * h, 128 * (h + 1))
            pieces = jnp.concatenate([pb[rows, 0:128], pb[rows, 128:256]], axis=0)
            out = jnp.dot(perm2[...], pieces, preferred_element_type=F32)
            dsend[c, 32 * h : 32 * (h + 1)] = out.reshape(32, 8, 128).astype(BF16)
        d_send(c)

    product(0)
    product(1)
    b_ring[3][1]()
    product(2)
    product(3)

    def p_copy(d):
        return pltpu.make_async_remote_copy(
            part.at[r], part.at[r], p_s.at[d - 1], p_r.at[d - 1],
            device_id={"rep": (r + d) % 4}, device_id_type=MESH,
        )

    for d in (1, 2, 3):
        p_copy(d).start()
    stats(right, False)
    stats(across, False)
    for d in (1, 2, 3):
        p_copy(d).wait_recv()
    entries = float(BLK * BLK)
    sums = part[0] + part[1] + part[2] + part[3]
    d_sq = jnp.sum(jnp.sum(sums[0], axis=0, keepdims=True), axis=1, keepdims=True)
    g_sq = jnp.sum(jnp.sum(sums[1], axis=0, keepdims=True), axis=1, keepdims=True)
    scale = jnp.sqrt(g_sq / entries) * lax.rsqrt(d_sq / entries + 1e-06)
    row = jnp.broadcast_to(scale, (1, 128))
    sclsend[...] = row
    scl[f] = row

    def s_copy(i):
        return pltpu.make_async_remote_copy(
            sclsend, scl.at[f], s_s.at[0], s_r.at[0],
            device_id={"fsdp": peer(i // LINE, i % LINE)}, device_id_type=MESH,
        )

    def s_start(i, carry):
        s_copy(i).start()
        return carry

    lax.fori_loop(1, NB, s_start, 0)
    l_o[...] = 0.95 * slbuf[...] + (0.05 / BLK) * l_o[...]
    r_o[...] = 0.95 * srbuf[...] + (0.05 / BLK) * r_o[...]

    for c in range(CH):
        pltpu.make_async_remote_copy(
            dsend.at[c, pl.ds(0, NB - 1)], dret.at[c, pl.ds(0, NB - 1)], d_s.at[c], d_r.at[c],
            device_id={"fsdp": peer(1, 0)}, device_id_type=MESH,
        ).wait()
    scales = pltpu.make_async_remote_copy(
        scl.at[pl.ds(0, NB - 1)], scl.at[pl.ds(0, NB - 1)], s_s.at[0], s_r.at[0],
        device_id={"fsdp": peer(1, 0)}, device_id_type=MESH,
    )
    scales.wait()

    def update(b, carry):
        s = own_ref[b]
        step = 0.2 * scl[s]
        d = jnp.concatenate([dret[c, s].astype(F32) for c in range(CH)], axis=0)
        z = zbuf[b] - step * d
        x = 0.75 * xbuf[b] + 0.25 * z
        z_o[b] = z
        x_o[b] = x
        y_o[b] = (0.1 * z + 0.9 * x).astype(BF16)
        return carry

    lax.fori_loop(0, NB, update, 0, unroll=4)

    pltpu.make_async_remote_copy(
        send.at[pl.ds(0, NB - 1)], held.at[pl.ds(0, NB - 1)], g_s.at[0], g_r.at[0],
        device_id={"fsdp": peer(1, 0)}, device_id_type=MESH,
    ).wait_send()
    for n in range(4):
        b_ring[n][3]()
        g_ring[n][3]()
    for d in (1, 2, 3):
        p_copy(d).wait_send()


def write_kernel(z, x, y, l, r, z_o, x_o, y_o, l_o, r_o, sem):
    copies = [
        pltpu.make_async_copy(a, b, sem.at[n])
        for n, (a, b) in enumerate(((z, z_o), (x, x_o), (y, y_o), (l, l_o), (r, r_o)))
    ]
    for copy in copies:
        copy.start()
    for copy in copies:
        copy.wait()


def pieces_of(flat):
    return flat[0].reshape(4, 512, 128).transpose(1, 0, 2).reshape(NB, 32, 128)


def flat_of(pieces):
    return pieces.reshape(512, 4, 128).transpose(1, 0, 2).reshape(1, 4, 65536)


def per_device(grad, z_params, x_params, owner, stat_left, stat_right, root_left, root_right):
    slots = jnp.arange(NB, dtype=jnp.int32)
    inverse = jnp.sum(jnp.where(owner[None, :] == slots[:, None], slots[None, :], 0), axis=1)
    smem = pl.BlockSpec(memory_space=pltpu.SMEM)
    hbm = pl.BlockSpec(memory_space=pltpu.HBM)
    vmem = pl.BlockSpec(memory_space=pltpu.VMEM)
    anywhere = pl.BlockSpec(memory_space=pl.ANY)
    shapes = (
        ((NB, 32, 128), F32),
        ((NB, 32, 128), F32),
        ((NB, 32, 128), BF16),
        ((Q, BLK), F32),
        ((Q, BLK), F32),
    )
    dma = pltpu.SemaphoreType.DMA
    results = pl.pallas_call(
        remote_kernel,
        out_shape=tuple(pltpu.VMEM(s, t) for s, t in shapes),
        in_specs=[smem, smem] + [hbm] * 7,
        out_specs=(vmem,) * 5,
        scratch_shapes=[
            pltpu.VMEM((NB, 32, 128), F32),
            pltpu.VMEM((NB, 32, 128), BF16),
            pltpu.VMEM((NB, 32, 128), BF16),
            pltpu.VMEM((4, Q, BLK), BF16),
            pltpu.VMEM((CH, 4, Q, Q), BF16),
            pltpu.VMEM((4, Q, Q), BF16),
            pltpu.VMEM((Q, BLK), F32),
            pltpu.VMEM((Q, BLK), BF16),
            pltpu.VMEM((NB, 32, 128), F32),
            pltpu.VMEM((NB, 32, 128), F32),
            pltpu.VMEM((Q, BLK), F32),
            pltpu.VMEM((Q, BLK), F32),
            pltpu.VMEM((Q, Q), BF16),
            pltpu.VMEM((Q, Q), BF16),
            pltpu.VMEM((CH, NB, 8, 128), BF16),
            pltpu.VMEM((CH, NB, 8, 128), BF16),
            pltpu.VMEM((4, 2, 8, 128), F32),
            pltpu.VMEM((NB, 1, 128), F32),
            pltpu.VMEM((1, 128), F32),
            dma((13,)),
            pltpu.SemaphoreType.REGULAR,
            dma((8, 2)),
            dma((8, 2)),
            dma((8, 2)),
            dma((8, 2)),
            dma((1,)),
            dma((4,)),
            dma((CH,)),
            dma((CH,)),
            dma((3,)),
            dma((3,)),
            dma((1,)),
            dma((1,)),
        ],
        compiler_params=pltpu.CompilerParams(
            collective_id=0, has_side_effects=True, vmem_limit_bytes=36 << 20
        ),
        name="shampoo",
    )(
        inverse, owner, pieces_of(grad), pieces_of(z_params), pieces_of(x_params),
        stat_left[0], stat_right[0], root_left[0], root_right[0],
    )
    z, x, y, left_new, right_new = pl.pallas_call(
        write_kernel,
        out_shape=tuple(jax.ShapeDtypeStruct(s, t) for s, t in shapes),
        in_specs=[vmem] * 5,
        out_specs=(anywhere,) * 5,
        scratch_shapes=[dma((5,))],
        compiler_params=pltpu.CompilerParams(vmem_limit_bytes=8 << 20),
        name="write",
    )(*results)
    return (flat_of(z), flat_of(x), flat_of(y), left_new[None], right_new[None])


def solution(mesh):
    return jax.shard_map(
        per_device,
        mesh=mesh,
        in_specs=(P("rep", "fsdp", None),) * 3 + (P(),) + (P("fsdp", "rep", None),) * 4,
        out_specs=(P("rep", "fsdp", None),) * 3 + (P("fsdp", "rep", None),) * 2,
        check_vma=False,
    )
```

```python
import functools

import jax
import jax.numpy as jnp
from jax import lax
from jax.experimental import pallas as pl
from jax.experimental.pallas import tpu as pltpu
from jax.sharding import PartitionSpec as P

MESH = pl.DeviceIdType.MESH
F32 = jnp.float32
BF16 = jnp.bfloat16

NB = 64
BLK = 1024
Q = 256
LINE = 16
CH = 4


def iota(shape, dim):
    return lax.broadcasted_iota(jnp.int32, shape, dim)


def fold(v):
    rows, cols = v.shape
    total = v[:, 0:128]
    for j in range(1, cols // 128):
        total = total + v[:, 128 * j : 128 * (j + 1)]
    return jnp.sum(total.reshape(rows // 8, 8, 128), axis=0)


def remote_kernel(
    inv_ref, own_ref, grad_ref, z_ref, x_ref, sl_ref, sr_ref, rl_ref, rr_ref,
    z_o, x_o, y_o, l_o, r_o,
    gbuf, send, held, gq, bc, ac, lg, lgb, zbuf, xbuf, slbuf, srbuf,
    perm1, perm2, dsend, dret, part, scl, sclsend,
    loc, line_sem, y_s1, y_s2, y_r1, y_r2, g_s, g_r, d_s, d_r, p_s, p_r, s_s, s_r,
):
    f = lax.axis_index("fsdp")
    r = lax.axis_index("rep")
    fx, fz, fc = f // LINE, (f % LINE) // 2, f % 2
    right, left, across = (r + 1) % 4, (r + 3) % 4, (r + 2) % 4

    def peer(j, i):
        return ((fx + j) % 4) * LINE + ((fz + i // 2) % 8) * 2 + (fc + i) % 2

    barrier = pltpu.get_barrier_semaphore()

    def greet(i, c):
        pl.semaphore_signal(barrier, inc=1, device_id={"fsdp": peer(0, i)}, device_id_type=MESH)
        return c

    lax.fori_loop(1, LINE, greet, 0)
    for d in (1, 2, 3):
        pl.semaphore_signal(barrier, inc=1, device_id={"fsdp": peer(d, 0)}, device_id_type=MESH)
        pl.semaphore_signal(barrier, inc=1, device_id={"rep": (r + d) % 4}, device_id_type=MESH)

    loads = [pltpu.make_async_copy(grad_ref, gbuf, loc.at[0])]
    for c in range(CH):
        loads.append(
            pltpu.make_async_copy(rr_ref.at[:, pl.ds(Q * c, Q)], bc.at[c, r], loc.at[1 + c])
        )
    for c in range(4):
        loads.append(
            pltpu.make_async_copy(rl_ref.at[:, pl.ds(Q * c, Q)], ac.at[c], loc.at[5 + c])
        )
    for n, (a, b) in enumerate(((sl_ref, slbuf), (sr_ref, srbuf), (z_ref, zbuf), (x_ref, xbuf))):
        loads.append(pltpu.make_async_copy(a, b, loc.at[9 + n]))
    for load in loads:
        load.start()

    o, i = iota((Q, Q), 0), iota((Q, Q), 1)
    perm1[...] = (((i % 32) // 4) * 32 + (i // 32) * 4 + i % 4 == o).astype(F32).astype(BF16)
    perm2[...] = (((i % 128) // 4) * 8 + (i // 128) * 4 + i % 4 == o).astype(F32).astype(BF16)

    loads[0].wait()

    def prepare(s, c):
        send[s] = gbuf[inv_ref[s]].astype(BF16)
        return c

    lax.fori_loop(0, NB, prepare, 0, unroll=4)
    held[f] = send[f]
    for c in range(CH):
        loads[1 + c].wait()

    def ring(n, ref, sub, half0, half1):
        def first():
            for side, to in ((0, right), (1, left)):
                pltpu.make_async_remote_copy(
                    sub(ref, r), sub(ref, r), y_s1.at[n, side], y_r1.at[n, side],
                    device_id={"rep": to}, device_id_type=MESH,
                ).start()

        def second():
            for side, to, frm, half in ((0, right, left, half0), (1, left, right, half1)):
                pltpu.make_async_remote_copy(
                    sub(ref, frm), sub(ref, frm), y_s1.at[n, side], y_r1.at[n, side],
                    device_id={"rep": to}, device_id_type=MESH,
                ).wait_recv()
                pltpu.make_async_remote_copy(
                    half(ref, frm), half(ref, frm), y_s2.at[n, side], y_r2.at[n, side],
                    device_id={"rep": to}, device_id_type=MESH,
                ).start()

        def done():
            for side, to, half in ((0, right, half0), (1, left, half1)):
                pltpu.make_async_remote_copy(
                    half(ref, across), half(ref, across), y_s2.at[n, side], y_r2.at[n, side],
                    device_id={"rep": to}, device_id_type=MESH,
                ).wait_recv()

        def drain():
            for side, to, half in ((0, right, half0), (1, left, half1)):
                pltpu.make_async_remote_copy(
                    sub(ref, r), sub(ref, r), y_s1.at[n, side], y_r1.at[n, side],
                    device_id={"rep": to}, device_id_type=MESH,
                ).wait_send()
                pltpu.make_async_remote_copy(
                    half(ref, r), half(ref, r), y_s2.at[n, side], y_r2.at[n, side],
                    device_id={"rep": to}, device_id_type=MESH,
                ).wait_send()

        return first, second, done, drain

    def rows_of(start, size):
        return lambda ref, k: ref.at[k, pl.ds(start, size)]

    b_ring = [
        ring(c, bc.at[c], rows_of(0, Q), rows_of(0, Q // 2), rows_of(Q // 2, Q // 2))
        for c in range(CH)
    ]
    g_ring = []
    for j in range(4):
        base = pl.multiple_of(((fx + 4 - j) % 4) * 64, 64)
        g_ring.append(
            ring(4 + j, gq, rows_of(base, 64), rows_of(base, 32), rows_of(base + 32, 32))
        )

    def g_copy(j, i):
        to = peer(j, i)
        return pltpu.make_async_remote_copy(
            send.at[to], held.at[f], g_s.at[0], g_r.at[j],
            device_id={"fsdp": to}, device_id_type=MESH,
        )

    def g_send(j):
        def body(i, c):
            g_copy(j, i).start()
            return c

        lax.fori_loop(1 if j == 0 else 0, LINE, body, 0)

    def g_take(j):
        count = 15 if j == 0 else 16
        pltpu.make_async_remote_copy(
            send.at[pl.ds(0, count)], held.at[pl.ds(0, count)], g_s.at[0], g_r.at[j],
            device_id={"fsdp": peer(1, 0)}, device_id_type=MESH,
        ).wait_recv()
        line = (fx + 4 - j) % 4
        pieces = jnp.concatenate(
            [held[pl.ds(line * LINE + 8 * h, 8)].reshape(Q, 128) for h in range(2)], axis=1
        )
        rows = jnp.dot(perm1[...], pieces, preferred_element_type=F32).astype(BF16)
        for h in range(2):
            at = pl.multiple_of(line * 64 + 32 * h, 32)
            for t in range(8):
                gq[r, pl.ds(at, 32), 128 * t : 128 * (t + 1)] = rows[
                    32 * t : 32 * (t + 1), 128 * h : 128 * (h + 1)
                ]

    pl.semaphore_wait(barrier, 21)
    for d in (1, 2, 3):
        pl.semaphore_signal(line_sem, inc=1, device_id={"fsdp": peer(d, 0)}, device_id_type=MESH)
    g_send(0)
    b_ring[0][0]()
    b_ring[1][0]()
    pl.semaphore_wait(line_sem, 3)
    for j in range(1, 4):
        g_send(j)

    for load in loads[5:]:
        load.wait()

    def left_root(k, first):
        gk = gq.at[k]
        for n in range(4):
            cols = slice(Q * n, Q * (n + 1))
            term = jnp.dot(ac[k], gk[:, cols], preferred_element_type=F32)
            lg[:, cols] = term if first else lg[:, cols] + term

    def stats(k, first):
        gk = gq.at[k]
        l_o[:, pl.ds(pl.multiple_of(k * Q, Q), Q)] = lax.dot_general(
            gq[r], gk[...], (((1,), (1,)), ((), ())), preferred_element_type=F32
        )
        strip = gk[:, pl.ds(pl.multiple_of(r * Q, Q), Q)]
        for n in range(4):
            cols = slice(Q * n, Q * (n + 1))
            term = lax.dot_general(
                strip, gk[:, cols], (((0,), (0,)), ((), ())), preferred_element_type=F32
            )
            r_o[:, cols] = term if first else r_o[:, cols] + term

    b_ring[0][1]()
    g_take(0)
    g_ring[0][0]()
    b_ring[1][1]()
    g_take(1)
    g_ring[1][0]()
    g_ring[0][1]()
    g_take(2)
    g_ring[2][0]()
    g_ring[1][1]()
    g_take(3)
    g_ring[3][0]()
    b_ring[2][0]()
    own = gq[r].astype(F32)
    part[r, 1] = fold(own * own)
    left_root(r, True)
    stats(r, True)
    g_ring[2][1]()
    g_ring[3][1]()
    b_ring[3][0]()
    left_root(left, False)
    left_root(right, False)
    b_ring[2][1]()
    stats(left, False)
    for n in range(4):
        g_ring[n][2]()
    left_root(across, False)
    lgb[...] = lg[...].astype(BF16)

    def d_send(c):
        def body(i, carry):
            to = peer(i // LINE, i % LINE)
            pltpu.make_async_remote_copy(
                dsend.at[c, to], dret.at[c, f], d_s.at[c], d_r.at[c],
                device_id={"fsdp": to}, device_id_type=MESH,
            ).start()
            return carry

        lax.fori_loop(1, NB, body, 0)
        dret[c, f] = dsend[c, f]

    def product(c):
        b_ring[c][2]()
        p = jnp.dot(lgb[...], bc[c].reshape(BLK, Q), preferred_element_type=F32)
        squares = fold(p * p)
        part[r, 0] = squares if c == 0 else part[r, 0] + squares
        pb = p.astype(BF16)
        for h in range(2):
            rows = slice(128 * h, 128 * (h + 1))
            pieces = jnp.concatenate([pb[rows, 0:128], pb[rows, 128:256]], axis=0)
            out = jnp.dot(perm2[...], pieces, preferred_element_type=F32)
            dsend[c, 32 * h : 32 * (h + 1)] = out.reshape(32, 8, 128).astype(BF16)
        d_send(c)

    product(0)
    product(1)
    b_ring[3][1]()
    product(2)
    product(3)

    def p_copy(d):
        return pltpu.make_async_remote_copy(
            part.at[r], part.at[r], p_s.at[d - 1], p_r.at[d - 1],
            device_id={"rep": (r + d) % 4}, device_id_type=MESH,
        )

    for d in (1, 2, 3):
        p_copy(d).start()
    stats(right, False)
    stats(across, False)
    for d in (1, 2, 3):
        p_copy(d).wait_recv()
    entries = float(BLK * BLK)
    sums = part[0] + part[1] + part[2] + part[3]
    d_sq = jnp.sum(jnp.sum(sums[0], axis=0, keepdims=True), axis=1, keepdims=True)
    g_sq = jnp.sum(jnp.sum(sums[1], axis=0, keepdims=True), axis=1, keepdims=True)
    scale = jnp.sqrt(g_sq / entries) * lax.rsqrt(d_sq / entries + 1e-06)
    row = jnp.broadcast_to(scale, (1, 128))
    sclsend[...] = row
    scl[f] = row

    def s_copy(i):
        return pltpu.make_async_remote_copy(
            sclsend, scl.at[f], s_s.at[0], s_r.at[0],
            device_id={"fsdp": peer(i // LINE, i % LINE)}, device_id_type=MESH,
        )

    def s_start(i, carry):
        s_copy(i).start()
        return carry

    lax.fori_loop(1, NB, s_start, 0)
    l_o[...] = 0.95 * slbuf[...] + (0.05 / BLK) * l_o[...]
    r_o[...] = 0.95 * srbuf[...] + (0.05 / BLK) * r_o[...]

    for c in range(CH):
        pltpu.make_async_remote_copy(
            dsend.at[c, pl.ds(0, NB - 1)], dret.at[c, pl.ds(0, NB - 1)], d_s.at[c], d_r.at[c],
            device_id={"fsdp": peer(1, 0)}, device_id_type=MESH,
        ).wait()
    scales = pltpu.make_async_remote_copy(
        scl.at[pl.ds(0, NB - 1)], scl.at[pl.ds(0, NB - 1)], s_s.at[0], s_r.at[0],
        device_id={"fsdp": peer(1, 0)}, device_id_type=MESH,
    )
    scales.wait()

    def update(b, carry):
        s = own_ref[b]
        step = 0.2 * scl[s]
        d = jnp.concatenate([dret[c, s].astype(F32) for c in range(CH)], axis=0)
        z = zbuf[b] - step * d
        x = 0.75 * xbuf[b] + 0.25 * z
        z_o[b] = z
        x_o[b] = x
        y_o[b] = (0.1 * z + 0.9 * x).astype(BF16)
        return carry

    lax.fori_loop(0, NB, update, 0, unroll=4)

    pltpu.make_async_remote_copy(
        send.at[pl.ds(0, NB - 1)], held.at[pl.ds(0, NB - 1)], g_s.at[0], g_r.at[0],
        device_id={"fsdp": peer(1, 0)}, device_id_type=MESH,
    ).wait_send()
    for n in range(4):
        b_ring[n][3]()
        g_ring[n][3]()
    for d in (1, 2, 3):
        p_copy(d).wait_send()


def write_kernel(z, x, y, l, r, z_o, x_o, y_o, l_o, r_o, sem):
    copies = [
        pltpu.make_async_copy(a, b, sem.at[n])
        for n, (a, b) in enumerate(((z, z_o), (x, x_o), (y, y_o), (l, l_o), (r, r_o)))
    ]
    for copy in copies:
        copy.start()
    for copy in copies:
        copy.wait()


def pieces_of(flat):
    return flat[0].reshape(4, 512, 128).transpose(1, 0, 2).reshape(NB, 32, 128)


def flat_of(pieces):
    return pieces.reshape(512, 4, 128).transpose(1, 0, 2).reshape(1, 4, 65536)


def per_device(grad, z_params, x_params, owner, stat_left, stat_right, root_left, root_right):
    slots = jnp.arange(NB, dtype=jnp.int32)
    inverse = jnp.sum(jnp.where(owner[None, :] == slots[:, None], slots[None, :], 0), axis=1)
    smem = pl.BlockSpec(memory_space=pltpu.SMEM)
    vmem = pl.BlockSpec(memory_space=pltpu.VMEM)
    anywhere = pl.BlockSpec(memory_space=pl.ANY)
    shapes = (
        ((NB, 32, 128), F32),
        ((NB, 32, 128), F32),
        ((NB, 32, 128), BF16),
        ((Q, BLK), F32),
        ((Q, BLK), F32),
    )
    dma = pltpu.SemaphoreType.DMA
    results = pl.pallas_call(
        remote_kernel,
        out_shape=tuple(pltpu.VMEM(s, t) for s, t in shapes),
        in_specs=[smem, smem] + [anywhere] * 7,
        out_specs=(vmem,) * 5,
        scratch_shapes=[
            pltpu.VMEM((NB, 32, 128), F32),
            pltpu.VMEM((NB, 32, 128), BF16),
            pltpu.VMEM((NB, 32, 128), BF16),
            pltpu.VMEM((4, Q, BLK), BF16),
            pltpu.VMEM((CH, 4, Q, Q), BF16),
            pltpu.VMEM((4, Q, Q), BF16),
            pltpu.VMEM((Q, BLK), F32),
            pltpu.VMEM((Q, BLK), BF16),
            pltpu.VMEM((NB, 32, 128), F32),
            pltpu.VMEM((NB, 32, 128), F32),
            pltpu.VMEM((Q, BLK), F32),
            pltpu.VMEM((Q, BLK), F32),
            pltpu.VMEM((Q, Q), BF16),
            pltpu.VMEM((Q, Q), BF16),
            pltpu.VMEM((CH, NB, 8, 128), BF16),
            pltpu.VMEM((CH, NB, 8, 128), BF16),
            pltpu.VMEM((4, 2, 8, 128), F32),
            pltpu.VMEM((NB, 1, 128), F32),
            pltpu.VMEM((1, 128), F32),
            dma((13,)),
            pltpu.SemaphoreType.REGULAR,
            dma((8, 2)),
            dma((8, 2)),
            dma((8, 2)),
            dma((8, 2)),
            dma((1,)),
            dma((4,)),
            dma((CH,)),
            dma((CH,)),
            dma((3,)),
            dma((3,)),
            dma((1,)),
            dma((1,)),
        ],
        compiler_params=pltpu.CompilerParams(
            collective_id=0, has_side_effects=True, vmem_limit_bytes=57 << 20
        ),
        name="shampoo",
    )(
        inverse, owner, pieces_of(grad), pieces_of(z_params), pieces_of(x_params),
        stat_left[0], stat_right[0], root_left[0], root_right[0],
    )
    z, x, y, left_new, right_new = pl.pallas_call(
        write_kernel,
        out_shape=tuple(jax.ShapeDtypeStruct(s, t) for s, t in shapes),
        in_specs=[vmem] * 5,
        out_specs=(anywhere,) * 5,
        scratch_shapes=[dma((5,))],
        compiler_params=pltpu.CompilerParams(vmem_limit_bytes=8 << 20),
        name="write",
    )(*results)
    return (flat_of(z), flat_of(x), flat_of(y), left_new[None], right_new[None])


def solution(mesh):
    return jax.shard_map(
        per_device,
        mesh=mesh,
        in_specs=(P("rep", "fsdp", None),) * 3 + (P(),) + (P("fsdp", "rep", None),) * 4,
        out_specs=(P("rep", "fsdp", None),) * 3 + (P("fsdp", "rep", None),) * 2,
        check_vma=False,
    )
```

```python
import functools

import jax
import jax.numpy as jnp
from jax import lax
from jax.experimental import pallas as pl
from jax.experimental.pallas import tpu as pltpu
from jax.sharding import PartitionSpec as P

MESH = pl.DeviceIdType.MESH
F32 = jnp.float32
BF16 = jnp.bfloat16

NB = 64
BLK = 1024
Q = 256
LINE = 16
GC = 8
CH = 4


def iota(shape, dim):
    return lax.broadcasted_iota(jnp.int32, shape, dim)


def fold(v):
    rows, cols = v.shape
    total = v[:, 0:128]
    for j in range(1, cols // 128):
        total = total + v[:, 128 * j : 128 * (j + 1)]
    return jnp.sum(total.reshape(rows // 8, 8, 128), axis=0)


def remote_kernel(
    own_ref, grad_ref, z_ref, x_ref, sl_ref, sr_ref, rl_ref, rr_ref,
    z_o, x_o, y_o, l_o, r_o,
    gbuf, send, held, gq, bc, ac, lg, lgb, zbuf, xbuf, slbuf, srbuf,
    perm1, perm2, dsend, dret, part, scl, sclsend, spread, invv, inv,
    loc, line_sem, core_sem, y_s1, y_s2, y_r1, y_r2, g_s, g_r, d_s, d_r, p_s, p_r, s_s, s_r,
):
    f = lax.axis_index("fsdp")
    r = lax.axis_index("rep")
    fx, fz, fc = f // LINE, (f % LINE) // 2, f % 2
    other = f + 1 - 2 * fc
    right, left, across = (r + 1) % 4, (r + 3) % 4, (r + 2) % 4

    def peer(j, h, i):
        z = ((fz // 4 + h) % 2) * 4 + (fz + i // 2) % 4
        return ((fx + j) % 4) * LINE + z * 2 + (fc + i) % 2

    def peer_of(n):
        return peer(n // LINE, (n // 8) % 2, n % 8)

    barrier = pltpu.get_barrier_semaphore()

    def greet(to):
        pl.semaphore_signal(barrier, inc=1, device_id=to, device_id_type=MESH)

    greet({"fsdp": other, "rep": r})
    for d in (1, 2, 3):
        greet({"fsdp": f - fc, "rep": (r + d) % 4})
    for d in range(1, 8):
        greet({"fsdp": fx * LINE + ((fz + d) % 8) * 2 + 1, "rep": r})
    for d in (1, 2, 3):
        greet({"fsdp": ((fx + d) % 4) * LINE + fz * 2 + 1, "rep": r})

    loads = []
    for c in range(CH):
        loads.append(
            pltpu.make_async_copy(rr_ref.at[:, pl.ds(Q * c, Q)], bc.at[c, r], loc.at[1 + c])
        )
    loads.append(pltpu.make_async_copy(grad_ref, gbuf, loc.at[0]))
    for c in range(4):
        loads.append(
            pltpu.make_async_copy(rl_ref.at[:, pl.ds(Q * c, Q)], ac.at[c], loc.at[5 + c])
        )
    for n, (a, b) in enumerate(((sl_ref, slbuf), (sr_ref, srbuf), (z_ref, zbuf), (x_ref, xbuf))):
        loads.append(pltpu.make_async_copy(a, b, loc.at[9 + n]))
    for load in loads:
        load.start()

    def spread_row(b, c):
        spread[pl.ds(b, 1), :] = jnp.full((1, 128), own_ref[b], jnp.int32)
        return c

    lax.fori_loop(0, NB, spread_row, 0, unroll=8)
    hits = jnp.where(spread[...] == iota((NB, 128), 1), iota((NB, 128), 0), 0)
    invv[...] = jnp.max(hits, axis=0, keepdims=True)
    to_smem = pltpu.make_async_copy(invv, inv, loc.at[13])
    to_smem.start()

    def ring(n, ref, sub, half0, half1):
        def copy(part_of, k, side, to, s_sem, r_sem):
            return pltpu.make_async_remote_copy(
                part_of(ref, k), part_of(ref, k), s_sem.at[n, side], r_sem.at[n, side],
                device_id={"rep": to}, device_id_type=MESH,
            )

        def first():
            for side, to in ((0, right), (1, left)):
                copy(sub, r, side, to, y_s1, y_r1).start()

        def second():
            for side, to, frm, half in ((0, right, left, half0), (1, left, right, half1)):
                copy(sub, frm, side, to, y_s1, y_r1).wait_recv()
                copy(half, frm, side, to, y_s2, y_r2).start()

        def done():
            for side, to, half in ((0, right, half0), (1, left, half1)):
                copy(half, across, side, to, y_s2, y_r2).wait_recv()

        def drain():
            for side, to, half in ((0, right, half0), (1, left, half1)):
                copy(sub, r, side, to, y_s1, y_r1).wait_send()
                copy(half, r, side, to, y_s2, y_r2).wait_send()

        return first, second, done, drain

    def rows_of(start, size):
        return lambda ref, k: ref.at[k, pl.ds(start, size)]

    b_ring = [
        ring(c, bc.at[c], rows_of(0, Q), rows_of(0, Q // 2), rows_of(Q // 2, Q // 2))
        for c in range(CH)
    ]

    def place(q):
        return ((fx + 4 - q // 2) % 4) * LINE + ((fz // 4 + q) % 2) * 8

    g_ring = []
    for q in range(GC):
        base = pl.multiple_of(place(q) * 4, 32)
        g_ring.append(
            ring(CH + q, gq, rows_of(base, 32), rows_of(base, 16), rows_of(base + 16, 16))
        )

    for c in range(CH):
        loads[c].wait()

    @pl.when(fc == 0)
    def _():
        pl.semaphore_wait(barrier, 7)
        pl.semaphore_signal(
            core_sem, inc=1, device_id={"fsdp": other, "rep": r}, device_id_type=MESH
        )

    @pl.when(fc == 1)
    def _():
        pl.semaphore_wait(core_sem, 1)

    for c in range(2):
        b_ring[c][0]()

    o, i = iota((Q, Q), 0), iota((Q, Q), 1)
    perm1[...] = (((i % 32) // 4) * 32 + (i // 32) * 4 + i % 4 == o).astype(F32).astype(BF16)
    perm2[...] = (((i % 128) // 4) * 8 + (i // 128) * 4 + i % 4 == o).astype(F32).astype(BF16)

    to_smem.wait()
    loads[4].wait()

    def prepare(s, c):
        send[s] = gbuf[inv[0, s]].astype(BF16)
        return c

    lax.fori_loop(0, NB, prepare, 0, unroll=8)
    held[f] = send[f]

    def g_send(q):
        def body(n, c):
            to = peer_of(n)
            pltpu.make_async_remote_copy(
                send.at[to], held.at[f], g_s.at[0], g_r.at[q],
                device_id={"fsdp": to}, device_id_type=MESH,
            ).start()
            return c

        lax.fori_loop(1 if q == 0 else 8 * q, 8 * q + 8, body, 0)

    def g_take(q):
        count = 7 if q == 0 else 8
        pltpu.make_async_remote_copy(
            send.at[pl.ds(0, count)], held.at[pl.ds(0, count)], g_s.at[0], g_r.at[q],
            device_id={"fsdp": other}, device_id_type=MESH,
        ).wait_recv()
        at = place(q)
        pieces = held[pl.ds(at, 8)].reshape(Q, 128)
        rows = jnp.dot(perm1[...], pieces, preferred_element_type=F32).astype(BF16)
        base = pl.multiple_of(at * 4, 32)
        for t in range(8):
            gq[r, pl.ds(base, 32), 128 * t : 128 * (t + 1)] = rows[32 * t : 32 * (t + 1)]

    @pl.when(fc == 1)
    def _():
        pl.semaphore_wait(barrier, 21)
        pl.semaphore_signal(
            core_sem, inc=1, device_id={"fsdp": other, "rep": r}, device_id_type=MESH
        )

    @pl.when(fc == 0)
    def _():
        pl.semaphore_wait(core_sem, 1)

    for d in (1, 2, 3):
        pl.semaphore_signal(
            line_sem, inc=1, device_id={"fsdp": peer(d, 0, 0)}, device_id_type=MESH
        )
    g_send(0)
    g_send(1)
    pl.semaphore_wait(line_sem, 3)
    for q in range(2, GC):
        g_send(q)

    for load in loads[5:]:
        load.wait()

    def left_root(k, first):
        gk = gq.at[k]
        for n in range(4):
            cols = slice(Q * n, Q * (n + 1))
            term = jnp.dot(ac[k], gk[:, cols], preferred_element_type=F32)
            lg[:, cols] = term if first else lg[:, cols] + term

    def stats(k, first):
        gk = gq.at[k]
        l_o[:, pl.ds(pl.multiple_of(k * Q, Q), Q)] = lax.dot_general(
            gq[r], gk[...], (((1,), (1,)), ((), ())), preferred_element_type=F32
        )
        strip = gk[:, pl.ds(pl.multiple_of(r * Q, Q), Q)]
        for n in range(4):
            cols = slice(Q * n, Q * (n + 1))
            term = lax.dot_general(
                strip, gk[:, cols], (((0,), (0,)), ((), ())), preferred_element_type=F32
            )
            r_o[:, cols] = term if first else r_o[:, cols] + term

    b_ring[0][1]()
    b_ring[1][1]()
    for q in range(GC):
        g_take(q)
        g_ring[q][0]()
        if q >= 2:
            g_ring[q - 2][1]()
    g_ring[GC - 2][1]()
    left_root(r, True)
    g_ring[GC - 1][1]()
    b_ring[2][0]()
    b_ring[3][0]()
    left_root(left, False)
    left_root(right, False)
    own = gq[r].astype(F32)
    part[r, 1] = fold(own * own)
    for q in range(GC):
        g_ring[q][2]()
    left_root(across, False)
    lgb[...] = lg[...].astype(BF16)

    def p_copy(d):
        return pltpu.make_async_remote_copy(
            part.at[r], part.at[r], p_s.at[d - 1], p_r.at[d - 1],
            device_id={"rep": (r + d) % 4}, device_id_type=MESH,
        )

    def product(c):
        b_ring[c][2]()
        p = jnp.dot(lgb[...], bc[c].reshape(BLK, Q), preferred_element_type=F32)
        squares = fold(p * p)
        part[r, 0] = squares if c == 0 else part[r, 0] + squares
        if c == CH - 1:
            for d in (1, 2, 3):
                p_copy(d).start()
        pb = p.astype(BF16)
        for h in range(2):
            rows = slice(128 * h, 128 * (h + 1))
            pieces = jnp.concatenate([pb[rows, 0:128], pb[rows, 128:256]], axis=0)
            out = jnp.dot(perm2[...], pieces, preferred_element_type=F32)
            dsend[c // 2, 32 * h : 32 * (h + 1), c % 2] = out.reshape(32, 8, 128).astype(BF16)

    def d_send(p):
        def body(n, carry):
            to = peer_of(n)
            pltpu.make_async_remote_copy(
                dsend.at[p, to], dret.at[p, f], d_s.at[p], d_r.at[p],
                device_id={"fsdp": to}, device_id_type=MESH,
            ).start()
            return carry

        lax.fori_loop(1, NB, body, 0)
        dret[p, f] = dsend[p, f]

    product(0)
    product(1)
    d_send(0)
    b_ring[2][1]()
    stats(r, True)
    b_ring[3][1]()
    product(2)
    product(3)
    d_send(1)
    stats(left, False)
    stats(right, False)
    for d in (1, 2, 3):
        p_copy(d).wait_recv()
    entries = float(BLK * BLK)
    sums = part[0] + part[1] + part[2] + part[3]
    d_sq = jnp.sum(jnp.sum(sums[0], axis=0, keepdims=True), axis=1, keepdims=True)
    g_sq = jnp.sum(jnp.sum(sums[1], axis=0, keepdims=True), axis=1, keepdims=True)
    scale = jnp.sqrt(g_sq / entries) * lax.rsqrt(d_sq / entries + 1e-06)
    row = jnp.broadcast_to(scale, (1, 128))
    sclsend[...] = row
    scl[f] = row

    def s_start(n, carry):
        pltpu.make_async_remote_copy(
            sclsend, scl.at[f], s_s.at[0], s_r.at[0],
            device_id={"fsdp": peer_of(n)}, device_id_type=MESH,
        ).start()
        return carry

    lax.fori_loop(1, NB, s_start, 0)
    stats(across, False)
    l_o[...] = 0.95 * slbuf[...] + (0.05 / BLK) * l_o[...]
    r_o[...] = 0.95 * srbuf[...] + (0.05 / BLK) * r_o[...]

    pltpu.make_async_remote_copy(
        scl.at[pl.ds(0, NB - 1)], scl.at[pl.ds(0, NB - 1)], s_s.at[0], s_r.at[0],
        device_id={"fsdp": other}, device_id_type=MESH,
    ).wait()
    for p in range(2):
        pltpu.make_async_remote_copy(
            dsend.at[p, pl.ds(0, NB - 1)], dret.at[p, pl.ds(0, NB - 1)], d_s.at[p], d_r.at[p],
            device_id={"fsdp": other}, device_id_type=MESH,
        ).wait()

    def update(b, carry):
        s = own_ref[b]
        step = 0.2 * scl[s]
        for c in range(CH):
            z = zbuf[b, c] - step * dret[c // 2, s, c % 2].astype(F32)
            x = 0.75 * xbuf[b, c] + 0.25 * z
            z_o[b, c] = z
            x_o[b, c] = x
            y_o[b, c] = (0.1 * z + 0.9 * x).astype(BF16)
        return carry

    lax.fori_loop(0, NB, update, 0, unroll=4)

    pltpu.make_async_remote_copy(
        send.at[pl.ds(0, NB - 1)], held.at[pl.ds(0, NB - 1)], g_s.at[0], g_r.at[0],
        device_id={"fsdp": other}, device_id_type=MESH,
    ).wait_send()
    for chunk in b_ring + g_ring:
        chunk[3]()
    for d in (1, 2, 3):
        p_copy(d).wait_send()


def write_kernel(z, x, y, l, r, z_o, x_o, y_o, l_o, r_o, sem):
    copies = [
        pltpu.make_async_copy(a, b, sem.at[n])
        for n, (a, b) in enumerate(((z, z_o), (x, x_o), (y, y_o), (l, l_o), (r, r_o)))
    ]
    for copy in copies:
        copy.start()
    for copy in copies:
        copy.wait()


def pieces_of(flat):
    return flat[0].reshape(4, 512, 128).transpose(1, 0, 2).reshape(NB, CH, 8, 128)


def flat_of(pieces):
    return pieces.reshape(512, 4, 128).transpose(1, 0, 2).reshape(1, 4, 65536)


def per_device(grad, z_params, x_params, owner, stat_left, stat_right, root_left, root_right):
    smem = pl.BlockSpec(memory_space=pltpu.SMEM)
    vmem = pl.BlockSpec(memory_space=pltpu.VMEM)
    anywhere = pl.BlockSpec(memory_space=pl.ANY)
    shapes = (
        ((NB, CH, 8, 128), F32),
        ((NB, CH, 8, 128), F32),
        ((NB, CH, 8, 128), BF16),
        ((Q, BLK), F32),
        ((Q, BLK), F32),
    )
    dma = pltpu.SemaphoreType.DMA
    results = pl.pallas_call(
        remote_kernel,
        out_shape=tuple(pltpu.VMEM(s, t) for s, t in shapes),
        in_specs=[smem] + [anywhere] * 7,
        out_specs=(vmem,) * 5,
        scratch_shapes=[
            pltpu.VMEM((NB, 32, 128), F32),
            pltpu.VMEM((NB, 32, 128), BF16),
            pltpu.VMEM((NB, 32, 128), BF16),
            pltpu.VMEM((4, Q, BLK), BF16),
            pltpu.VMEM((CH, 4, Q, Q), BF16),
            pltpu.VMEM((4, Q, Q), BF16),
            pltpu.VMEM((Q, BLK), F32),
            pltpu.VMEM((Q, BLK), BF16),
            pltpu.VMEM((NB, CH, 8, 128), F32),
            pltpu.VMEM((NB, CH, 8, 128), F32),
            pltpu.VMEM((Q, BLK), F32),
            pltpu.VMEM((Q, BLK), F32),
            pltpu.VMEM((Q, Q), BF16),
            pltpu.VMEM((Q, Q), BF16),
            pltpu.VMEM((2, NB, 2, 8, 128), BF16),
            pltpu.VMEM((2, NB, 2, 8, 128), BF16),
            pltpu.VMEM((4, 2, 8, 128), F32),
            pltpu.VMEM((NB, 1, 128), F32),
            pltpu.VMEM((1, 128), F32),
            pltpu.VMEM((NB, 128), jnp.int32),
            pltpu.VMEM((1, 128), jnp.int32),
            pltpu.SMEM((1, 128), jnp.int32),
            dma((14,)),
            pltpu.SemaphoreType.REGULAR,
            pltpu.SemaphoreType.REGULAR,
            dma((CH + GC, 2)),
            dma((CH + GC, 2)),
            dma((CH + GC, 2)),
            dma((CH + GC, 2)),
            dma((1,)),
            dma((GC,)),
            dma((2,)),
            dma((2,)),
            dma((3,)),
            dma((3,)),
            dma((1,)),
            dma((1,)),
        ],
        compiler_params=pltpu.CompilerParams(
            collective_id=0, has_side_effects=True, vmem_limit_bytes=57 << 20
        ),
        name="shampoo",
    )(
        owner, pieces_of(grad).reshape(NB, 32, 128), pieces_of(z_params), pieces_of(x_params),
        stat_left[0], stat_right[0], root_left[0], root_right[0],
    )
    z, x, y, left_new, right_new = pl.pallas_call(
        write_kernel,
        out_shape=tuple(jax.ShapeDtypeStruct(s, t) for s, t in shapes),
        in_specs=[vmem] * 5,
        out_specs=(anywhere,) * 5,
        scratch_shapes=[dma((5,))],
        compiler_params=pltpu.CompilerParams(vmem_limit_bytes=8 << 20),
        name="write",
    )(*results)
    return (flat_of(z), flat_of(x), flat_of(y), left_new[None], right_new[None])


def solution(mesh):
    return jax.shard_map(
        per_device,
        mesh=mesh,
        in_specs=(P("rep", "fsdp", None),) * 3 + (P(),) + (P("fsdp", "rep", None),) * 4,
        out_specs=(P("rep", "fsdp", None),) * 3 + (P("fsdp", "rep", None),) * 2,
        check_vma=False,
    )
```

```python
import functools

import jax
import jax.numpy as jnp
from jax import lax
from jax.experimental import pallas as pl
from jax.experimental.pallas import tpu as pltpu
from jax.sharding import PartitionSpec as P

MESH = pl.DeviceIdType.MESH
F32 = jnp.float32
BF16 = jnp.bfloat16

NB = 64
BLK = 1024
Q = 256
LINE = 16
GC = 8
CH = 4


def iota(shape, dim):
    return lax.broadcasted_iota(jnp.int32, shape, dim)


def fold(v):
    rows, cols = v.shape
    total = v[:, 0:128]
    for j in range(1, cols // 128):
        total = total + v[:, 128 * j : 128 * (j + 1)]
    return jnp.sum(total.reshape(rows // 8, 8, 128), axis=0)


def remote_kernel(
    own_hbm, grad_ref, z_ref, x_ref, sl_ref, sr_ref, rl_ref, rr_ref,
    z_o, x_o, y_o, l_o, r_o,
    gbuf, send, held, gq, bc, ac, lg, lgb, zbuf, xbuf, slbuf, srbuf,
    perm1, perm2, dsend, dret, part, scl, sclsend, spread, invv, inv, own_ref,
    loc, line_sem, core_sem, y_s1, y_s2, y_r1, y_r2, g_s, g_r, d_s, d_r, p_s, p_r, s_s, s_r,
):
    f = lax.axis_index("fsdp")
    r = lax.axis_index("rep")
    fx, fz, fc = f // LINE, (f % LINE) // 2, f % 2
    other = f + 1 - 2 * fc
    right, left, across = (r + 1) % 4, (r + 3) % 4, (r + 2) % 4

    def peer(j, h, i):
        z = ((fz // 4 + h) % 2) * 4 + (fz + i // 2) % 4
        return ((fx + j) % 4) * LINE + z * 2 + (fc + i) % 2

    def peer_of(n):
        return peer(n // LINE, (n // 8) % 2, n % 8)

    barrier = pltpu.get_barrier_semaphore()

    def greet(to):
        pl.semaphore_signal(barrier, inc=1, device_id=to, device_id_type=MESH)

    greet({"fsdp": other, "rep": r})
    for d in (1, 2, 3):
        greet({"fsdp": f - fc, "rep": (r + d) % 4})
    for d in range(1, 8):
        greet({"fsdp": fx * LINE + ((fz + d) % 8) * 2 + 1, "rep": r})
    for d in (1, 2, 3):
        greet({"fsdp": ((fx + d) % 4) * LINE + fz * 2 + 1, "rep": r})

    owners = pltpu.make_async_copy(own_hbm, own_ref, loc.at[14])
    owners.start()
    loads = []
    for c in range(CH):
        loads.append(
            pltpu.make_async_copy(rr_ref.at[:, pl.ds(Q * c, Q)], bc.at[c, r], loc.at[1 + c])
        )
    loads.append(pltpu.make_async_copy(grad_ref, gbuf, loc.at[0]))
    for c in range(4):
        loads.append(
            pltpu.make_async_copy(rl_ref.at[:, pl.ds(Q * c, Q)], ac.at[c], loc.at[5 + c])
        )
    for n, (a, b) in enumerate(((sl_ref, slbuf), (sr_ref, srbuf), (z_ref, zbuf), (x_ref, xbuf))):
        loads.append(pltpu.make_async_copy(a, b, loc.at[9 + n]))
    for load in loads:
        load.start()

    owners.wait()

    def spread_row(b, c):
        spread[pl.ds(b, 1), :] = jnp.full((1, 128), own_ref[b], jnp.int32)
        return c

    lax.fori_loop(0, NB, spread_row, 0, unroll=8)
    hits = jnp.where(spread[...] == iota((NB, 128), 1), iota((NB, 128), 0), 0)
    invv[...] = jnp.max(hits, axis=0, keepdims=True)
    to_smem = pltpu.make_async_copy(invv, inv, loc.at[13])
    to_smem.start()

    def ring(n, ref, sub, half0, half1):
        def copy(part_of, k, side, to, s_sem, r_sem):
            return pltpu.make_async_remote_copy(
                part_of(ref, k), part_of(ref, k), s_sem.at[n, side], r_sem.at[n, side],
                device_id={"rep": to}, device_id_type=MESH,
            )

        def first():
            for side, to in ((0, right), (1, left)):
                copy(sub, r, side, to, y_s1, y_r1).start()

        def second():
            for side, to, frm, half in ((0, right, left, half0), (1, left, right, half1)):
                copy(sub, frm, side, to, y_s1, y_r1).wait_recv()
                copy(half, frm, side, to, y_s2, y_r2).start()

        def done():
            for side, to, half in ((0, right, half0), (1, left, half1)):
                copy(half, across, side, to, y_s2, y_r2).wait_recv()

        def drain():
            for side, to, half in ((0, right, half0), (1, left, half1)):
                copy(sub, r, side, to, y_s1, y_r1).wait_send()
                copy(half, r, side, to, y_s2, y_r2).wait_send()

        return first, second, done, drain

    def rows_of(start, size):
        return lambda ref, k: ref.at[k, pl.ds(start, size)]

    b_ring = [
        ring(c, bc.at[c], rows_of(0, Q), rows_of(0, Q // 2), rows_of(Q // 2, Q // 2))
        for c in range(CH)
    ]

    def place(q):
        return ((fx + 4 - q // 2) % 4) * LINE + ((fz // 4 + q) % 2) * 8

    g_ring = []
    for q in range(GC):
        base = pl.multiple_of(place(q) * 4, 32)
        g_ring.append(
            ring(CH + q, gq, rows_of(base, 32), rows_of(base, 16), rows_of(base + 16, 16))
        )

    for c in range(CH):
        loads[c].wait()

    @pl.when(fc == 0)
    def _():
        pl.semaphore_wait(barrier, 7)
        pl.semaphore_signal(
            core_sem, inc=1, device_id={"fsdp": other, "rep": r}, device_id_type=MESH
        )

    @pl.when(fc == 1)
    def _():
        pl.semaphore_wait(core_sem, 1)

    for c in range(2):
        b_ring[c][0]()

    o, i = iota((Q, Q), 0), iota((Q, Q), 1)
    perm1[...] = (((i % 32) // 4) * 32 + (i // 32) * 4 + i % 4 == o).astype(F32).astype(BF16)
    perm2[...] = (((i % 128) // 4) * 8 + (i // 128) * 4 + i % 4 == o).astype(F32).astype(BF16)

    to_smem.wait()
    loads[4].wait()

    def prepare(s, c):
        send[s] = gbuf[inv[0, s]].astype(BF16)
        return c

    lax.fori_loop(0, NB, prepare, 0, unroll=8)
    held[f] = send[f]

    def g_send(q):
        def body(n, c):
            to = peer_of(n)
            pltpu.make_async_remote_copy(
                send.at[to], held.at[f], g_s.at[0], g_r.at[q],
                device_id={"fsdp": to}, device_id_type=MESH,
            ).start()
            return c

        lax.fori_loop(1 if q == 0 else 8 * q, 8 * q + 8, body, 0, unroll=True)

    def g_take(q):
        count = 7 if q == 0 else 8
        pltpu.make_async_remote_copy(
            send.at[pl.ds(0, count)], held.at[pl.ds(0, count)], g_s.at[0], g_r.at[q],
            device_id={"fsdp": other}, device_id_type=MESH,
        ).wait_recv()
        at = place(q)
        pieces = held[pl.ds(at, 8)].reshape(Q, 128)
        rows = jnp.dot(perm1[...], pieces, preferred_element_type=F32).astype(BF16)
        base = pl.multiple_of(at * 4, 32)
        for t in range(8):
            gq[r, pl.ds(base, 32), 128 * t : 128 * (t + 1)] = rows[32 * t : 32 * (t + 1)]

    @pl.when(fc == 1)
    def _():
        pl.semaphore_wait(barrier, 21)
        pl.semaphore_signal(
            core_sem, inc=1, device_id={"fsdp": other, "rep": r}, device_id_type=MESH
        )

    @pl.when(fc == 0)
    def _():
        pl.semaphore_wait(core_sem, 1)

    for d in (1, 2, 3):
        pl.semaphore_signal(
            line_sem, inc=1, device_id={"fsdp": peer(d, 0, 0)}, device_id_type=MESH
        )
    g_send(0)
    g_send(1)
    pl.semaphore_wait(line_sem, 3)
    for q in range(2, 5):
        g_send(q)
    b_ring[0][1]()
    for q in range(5, GC):
        g_send(q)

    for load in loads[5:]:
        load.wait()

    def left_root(k, first):
        gk = gq.at[k]
        for n in range(4):
            cols = slice(Q * n, Q * (n + 1))
            term = jnp.dot(ac[k], gk[:, cols], preferred_element_type=F32)
            lg[:, cols] = term if first else lg[:, cols] + term

    def stats(k, first):
        gk = gq.at[k]
        l_o[:, pl.ds(pl.multiple_of(k * Q, Q), Q)] = lax.dot_general(
            gq[r], gk[...], (((1,), (1,)), ((), ())), preferred_element_type=F32
        )
        strip = gk[:, pl.ds(pl.multiple_of(r * Q, Q), Q)]
        for n in range(4):
            cols = slice(Q * n, Q * (n + 1))
            term = lax.dot_general(
                strip, gk[:, cols], (((0,), (0,)), ((), ())), preferred_element_type=F32
            )
            r_o[:, cols] = term if first else r_o[:, cols] + term

    b_ring[1][1]()
    for q in range(GC):
        g_take(q)
        g_ring[q][0]()
        if q >= 2:
            g_ring[q - 2][1]()
    g_ring[GC - 2][1]()
    left_root(r, True)
    g_ring[GC - 1][1]()
    b_ring[2][0]()
    b_ring[3][0]()
    left_root(left, False)
    left_root(right, False)
    own = gq[r].astype(F32)
    part[r, 1] = fold(own * own)
    for q in range(GC):
        g_ring[q][2]()
    left_root(across, False)
    lgb[...] = lg[...].astype(BF16)

    def p_copy(d):
        return pltpu.make_async_remote_copy(
            part.at[r], part.at[r], p_s.at[d - 1], p_r.at[d - 1],
            device_id={"rep": (r + d) % 4}, device_id_type=MESH,
        )

    def product(c):
        b_ring[c][2]()
        p = jnp.dot(lgb[...], bc[c].reshape(BLK, Q), preferred_element_type=F32)
        squares = fold(p * p)
        part[r, 0] = squares if c == 0 else part[r, 0] + squares
        if c == CH - 1:
            for d in (1, 2, 3):
                p_copy(d).start()
        pb = p.astype(BF16)
        for h in range(2):
            rows = slice(128 * h, 128 * (h + 1))
            pieces = jnp.concatenate([pb[rows, 0:128], pb[rows, 128:256]], axis=0)
            out = jnp.dot(perm2[...], pieces, preferred_element_type=F32)
            dsend[c // 2, 32 * h : 32 * (h + 1), c % 2] = out.reshape(32, 8, 128).astype(BF16)

    def d_send(p):
        def body(n, carry):
            to = peer_of(n)
            pltpu.make_async_remote_copy(
                dsend.at[p, to], dret.at[p, f], d_s.at[p], d_r.at[p],
                device_id={"fsdp": to}, device_id_type=MESH,
            ).start()
            return carry

        lax.fori_loop(1, NB, body, 0, unroll=9)
        dret[p, f] = dsend[p, f]

    product(0)
    product(1)
    d_send(0)
    b_ring[2][1]()
    stats(r, True)
    b_ring[3][1]()
    product(2)
    product(3)
    d_send(1)
    stats(left, False)
    stats(right, False)
    for d in (1, 2, 3):
        p_copy(d).wait_recv()
    entries = float(BLK * BLK)
    sums = part[0] + part[1] + part[2] + part[3]
    d_sq = jnp.sum(jnp.sum(sums[0], axis=0, keepdims=True), axis=1, keepdims=True)
    g_sq = jnp.sum(jnp.sum(sums[1], axis=0, keepdims=True), axis=1, keepdims=True)
    scale = jnp.sqrt(g_sq / entries) * lax.rsqrt(d_sq / entries + 1e-06)
    row = jnp.broadcast_to(scale, (1, 128))
    sclsend[...] = row
    scl[f] = row

    def s_start(n, carry):
        pltpu.make_async_remote_copy(
            sclsend, scl.at[f], s_s.at[0], s_r.at[0],
            device_id={"fsdp": peer_of(n)}, device_id_type=MESH,
        ).start()
        return carry

    lax.fori_loop(1, NB, s_start, 0, unroll=9)
    stats(across, False)
    l_o[...] = 0.95 * slbuf[...] + (0.05 / BLK) * l_o[...]
    r_o[...] = 0.95 * srbuf[...] + (0.05 / BLK) * r_o[...]

    pltpu.make_async_remote_copy(
        scl.at[pl.ds(0, NB - 1)], scl.at[pl.ds(0, NB - 1)], s_s.at[0], s_r.at[0],
        device_id={"fsdp": other}, device_id_type=MESH,
    ).wait()
    for p in range(2):
        pltpu.make_async_remote_copy(
            dsend.at[p, pl.ds(0, NB - 1)], dret.at[p, pl.ds(0, NB - 1)], d_s.at[p], d_r.at[p],
            device_id={"fsdp": other}, device_id_type=MESH,
        ).wait()

    def update(b, carry):
        s = own_ref[b]
        step = 0.2 * scl[s]
        for c in range(CH):
            z = zbuf[b, c] - step * dret[c // 2, s, c % 2].astype(F32)
            x = 0.75 * xbuf[b, c] + 0.25 * z
            z_o[b, c] = z
            x_o[b, c] = x
            y_o[b, c] = (0.1 * z + 0.9 * x).astype(BF16)
        return carry

    lax.fori_loop(0, NB, update, 0, unroll=4)

    pltpu.make_async_remote_copy(
        send.at[pl.ds(0, NB - 1)], held.at[pl.ds(0, NB - 1)], g_s.at[0], g_r.at[0],
        device_id={"fsdp": other}, device_id_type=MESH,
    ).wait_send()
    for chunk in b_ring + g_ring:
        chunk[3]()
    for d in (1, 2, 3):
        p_copy(d).wait_send()


def write_kernel(z, x, y, l, r, z_o, x_o, y_o, l_o, r_o, sem):
    copies = [
        pltpu.make_async_copy(a, b, sem.at[n])
        for n, (a, b) in enumerate(((z, z_o), (x, x_o), (y, y_o), (l, l_o), (r, r_o)))
    ]
    for copy in copies:
        copy.start()
    for copy in copies:
        copy.wait()


def pieces_of(flat):
    return flat[0].reshape(4, 512, 128).transpose(1, 0, 2).reshape(NB, CH, 8, 128)


def flat_of(pieces):
    return pieces.reshape(512, 4, 128).transpose(1, 0, 2).reshape(1, 4, 65536)


def per_device(grad, z_params, x_params, owner, stat_left, stat_right, root_left, root_right):
    vmem = pl.BlockSpec(memory_space=pltpu.VMEM)
    anywhere = pl.BlockSpec(memory_space=pl.ANY)
    shapes = (
        ((NB, CH, 8, 128), F32),
        ((NB, CH, 8, 128), F32),
        ((NB, CH, 8, 128), BF16),
        ((Q, BLK), F32),
        ((Q, BLK), F32),
    )
    dma = pltpu.SemaphoreType.DMA
    results = pl.pallas_call(
        remote_kernel,
        out_shape=tuple(pltpu.VMEM(s, t) for s, t in shapes),
        in_specs=[anywhere] * 8,
        out_specs=(vmem,) * 5,
        scratch_shapes=[
            pltpu.VMEM((NB, 32, 128), F32),
            pltpu.VMEM((NB, 32, 128), BF16),
            pltpu.VMEM((NB, 32, 128), BF16),
            pltpu.VMEM((4, Q, BLK), BF16),
            pltpu.VMEM((CH, 4, Q, Q), BF16),
            pltpu.VMEM((4, Q, Q), BF16),
            pltpu.VMEM((Q, BLK), F32),
            pltpu.VMEM((Q, BLK), BF16),
            pltpu.VMEM((NB, CH, 8, 128), F32),
            pltpu.VMEM((NB, CH, 8, 128), F32),
            pltpu.VMEM((Q, BLK), F32),
            pltpu.VMEM((Q, BLK), F32),
            pltpu.VMEM((Q, Q), BF16),
            pltpu.VMEM((Q, Q), BF16),
            pltpu.VMEM((2, NB, 2, 8, 128), BF16),
            pltpu.VMEM((2, NB, 2, 8, 128), BF16),
            pltpu.VMEM((4, 2, 8, 128), F32),
            pltpu.VMEM((NB, 1, 128), F32),
            pltpu.VMEM((1, 128), F32),
            pltpu.VMEM((NB, 128), jnp.int32),
            pltpu.VMEM((1, 128), jnp.int32),
            pltpu.SMEM((1, 128), jnp.int32),
            pltpu.SMEM((NB,), jnp.int32),
            dma((15,)),
            pltpu.SemaphoreType.REGULAR,
            pltpu.SemaphoreType.REGULAR,
            dma((CH + GC, 2)),
            dma((CH + GC, 2)),
            dma((CH + GC, 2)),
            dma((CH + GC, 2)),
            dma((1,)),
            dma((GC,)),
            dma((2,)),
            dma((2,)),
            dma((3,)),
            dma((3,)),
            dma((1,)),
            dma((1,)),
        ],
        compiler_params=pltpu.CompilerParams(
            collective_id=0, has_side_effects=True, vmem_limit_bytes=57 << 20
        ),
        name="shampoo",
    )(
        owner, pieces_of(grad).reshape(NB, 32, 128), pieces_of(z_params), pieces_of(x_params),
        stat_left[0], stat_right[0], root_left[0], root_right[0],
    )
    z, x, y, left_new, right_new = pl.pallas_call(
        write_kernel,
        out_shape=tuple(jax.ShapeDtypeStruct(s, t) for s, t in shapes),
        in_specs=[vmem] * 5,
        out_specs=(anywhere,) * 5,
        scratch_shapes=[dma((5,))],
        compiler_params=pltpu.CompilerParams(vmem_limit_bytes=8 << 20),
        name="write",
    )(*results)
    return (flat_of(z), flat_of(x), flat_of(y), left_new[None], right_new[None])


def solution(mesh):
    return jax.shard_map(
        per_device,
        mesh=mesh,
        in_specs=(P("rep", "fsdp", None),) * 3 + (P(),) + (P("fsdp", "rep", None),) * 4,
        out_specs=(P("rep", "fsdp", None),) * 3 + (P("fsdp", "rep", None),) * 2,
        check_vma=False,
    )
```

```python
import functools

import jax
import jax.numpy as jnp
from jax import lax
from jax.experimental import pallas as pl
from jax.experimental.pallas import tpu as pltpu
from jax.sharding import PartitionSpec as P

MESH = pl.DeviceIdType.MESH
F32 = jnp.float32
BF16 = jnp.bfloat16

NB = 64
BLK = 1024
Q = 256
LINE = 16
GC = 8
CH = 4


def iota(shape, dim):
    return lax.broadcasted_iota(jnp.int32, shape, dim)


def fold(v):
    rows, cols = v.shape
    total = v[:, 0:128]
    for j in range(1, cols // 128):
        total = total + v[:, 128 * j : 128 * (j + 1)]
    return jnp.sum(total.reshape(rows // 8, 8, 128), axis=0)


def remote_kernel(
    own_hbm, grad_ref, z_ref, x_ref, sl_ref, sr_ref, rl_ref, rr_ref,
    z_o, x_o, y_o, l_o, r_o,
    gbuf, send, held, gq, bc, ac, lg, lgb, zbuf, xbuf, slbuf, srbuf,
    perm1, perm2, dsend, dret, part, scl, sclsend, spread, invv, inv, own_ref,
    loc, line_sem, core_sem, y_s1, y_s2, y_r1, y_r2, g_s, g_r, d_s, d_r, p_s, p_r, s_s, s_r,
):
    f = lax.axis_index("fsdp")
    r = lax.axis_index("rep")
    fx, fz, fc = f // LINE, (f % LINE) // 2, f % 2
    other = f + 1 - 2 * fc
    right, left, across = (r + 1) % 4, (r + 3) % 4, (r + 2) % 4

    def peer(j, h, i):
        z = ((fz // 4 + h) % 2) * 4 + (fz + i // 2) % 4
        return ((fx + j) % 4) * LINE + z * 2 + (fc + i) % 2

    def peer_of(n):
        return peer(n // LINE, (n // 8) % 2, n % 8)

    barrier = pltpu.get_barrier_semaphore()

    def greet(to):
        pl.semaphore_signal(barrier, inc=1, device_id=to, device_id_type=MESH)

    greet({"fsdp": other, "rep": r})
    for d in (1, 2, 3):
        greet({"fsdp": f - fc, "rep": (r + d) % 4})
    for d in range(1, 8):
        greet({"fsdp": fx * LINE + ((fz + d) % 8) * 2 + 1, "rep": r})
    for d in (1, 2, 3):
        greet({"fsdp": ((fx + d) % 4) * LINE + fz * 2 + 1, "rep": r})

    owners = pltpu.make_async_copy(own_hbm, own_ref, loc.at[14])
    owners.start()
    loads = []
    for c in range(CH):
        loads.append(
            pltpu.make_async_copy(rr_ref.at[:, pl.ds(Q * c, Q)], bc.at[c, r], loc.at[1 + c])
        )
    loads.append(pltpu.make_async_copy(grad_ref, gbuf, loc.at[0]))
    for c in range(4):
        loads.append(
            pltpu.make_async_copy(rl_ref.at[:, pl.ds(Q * c, Q)], ac.at[c], loc.at[5 + c])
        )
    for n, (a, b) in enumerate(((sl_ref, slbuf), (sr_ref, srbuf), (z_ref, zbuf), (x_ref, xbuf))):
        loads.append(pltpu.make_async_copy(a, b, loc.at[9 + n]))
    for load in loads:
        load.start()

    owners.wait()

    def spread_row(b, c):
        spread[pl.ds(b, 1), :] = jnp.full((1, 128), own_ref[b], jnp.int32)
        return c

    lax.fori_loop(0, NB, spread_row, 0, unroll=8)
    hits = jnp.where(spread[...] == iota((NB, 128), 1), iota((NB, 128), 0), 0)
    invv[...] = jnp.max(hits, axis=0, keepdims=True)
    to_smem = pltpu.make_async_copy(invv, inv, loc.at[13])
    to_smem.start()

    def ring(n, ref, sub, half0, half1):
        def copy(part_of, k, side, to, s_sem, r_sem):
            return pltpu.make_async_remote_copy(
                part_of(ref, k), part_of(ref, k), s_sem.at[n, side], r_sem.at[n, side],
                device_id={"rep": to}, device_id_type=MESH,
            )

        def first():
            for side, to in ((0, right), (1, left)):
                copy(sub, r, side, to, y_s1, y_r1).start()

        def second():
            for side, to, frm, half in ((0, right, left, half0), (1, left, right, half1)):
                copy(sub, frm, side, to, y_s1, y_r1).wait_recv()
                copy(half, frm, side, to, y_s2, y_r2).start()

        def done():
            for side, to, half in ((0, right, half0), (1, left, half1)):
                copy(half, across, side, to, y_s2, y_r2).wait_recv()

        def drain():
            for side, to, half in ((0, right, half0), (1, left, half1)):
                copy(sub, r, side, to, y_s1, y_r1).wait_send()
                copy(half, r, side, to, y_s2, y_r2).wait_send()

        return first, second, done, drain

    def rows_of(start, size):
        return lambda ref, k: ref.at[k, pl.ds(start, size)]

    b_ring = [
        ring(c, bc.at[c], rows_of(0, Q), rows_of(0, Q // 2), rows_of(Q // 2, Q // 2))
        for c in range(CH)
    ]

    def place(q):
        return ((fx + 4 - q // 2) % 4) * LINE + ((fz // 4 + q) % 2) * 8

    g_ring = []
    for q in range(GC):
        base = pl.multiple_of(place(q) * 4, 32)
        g_ring.append(
            ring(CH + q, gq, rows_of(base, 32), rows_of(base, 16), rows_of(base + 16, 16))
        )

    for c in range(CH):
        loads[c].wait()

    @pl.when(fc == 0)
    def _():
        pl.semaphore_wait(barrier, 7)
        pl.semaphore_signal(
            core_sem, inc=1, device_id={"fsdp": other, "rep": r}, device_id_type=MESH
        )

    @pl.when(fc == 1)
    def _():
        pl.semaphore_wait(core_sem, 1)

    for c in range(2):
        b_ring[c][0]()

    o, i = iota((Q, Q), 0), iota((Q, Q), 1)
    perm1[...] = (((i % 32) // 4) * 32 + (i // 32) * 4 + i % 4 == o).astype(F32).astype(BF16)
    perm2[...] = (((i % 128) // 4) * 8 + (i // 128) * 4 + i % 4 == o).astype(F32).astype(BF16)

    to_smem.wait()
    loads[4].wait()

    def prepare(s, c):
        send[s] = gbuf[inv[0, s]].astype(BF16)
        return c

    lax.fori_loop(0, NB, prepare, 0, unroll=8)
    held[f] = send[f]

    def g_send(q):
        def body(n, c):
            to = peer_of(n)
            pltpu.make_async_remote_copy(
                send.at[to], held.at[f], g_s.at[0], g_r.at[q],
                device_id={"fsdp": to}, device_id_type=MESH,
            ).start()
            return c

        lax.fori_loop(1 if q == 0 else 8 * q, 8 * q + 8, body, 0, unroll=True)

    def g_take(q):
        count = 7 if q == 0 else 8
        pltpu.make_async_remote_copy(
            send.at[pl.ds(0, count)], held.at[pl.ds(0, count)], g_s.at[0], g_r.at[q],
            device_id={"fsdp": other}, device_id_type=MESH,
        ).wait_recv()
        at = place(q)
        pieces = held[pl.ds(at, 8)].reshape(Q, 128)
        rows = jnp.dot(perm1[...], pieces, preferred_element_type=F32).astype(BF16)
        base = pl.multiple_of(at * 4, 32)
        for t in range(8):
            gq[r, pl.ds(base, 32), 128 * t : 128 * (t + 1)] = rows[32 * t : 32 * (t + 1)]

    @pl.when(fc == 1)
    def _():
        pl.semaphore_wait(barrier, 21)
        pl.semaphore_signal(
            core_sem, inc=1, device_id={"fsdp": other, "rep": r}, device_id_type=MESH
        )

    @pl.when(fc == 0)
    def _():
        pl.semaphore_wait(core_sem, 1)

    for d in (1, 2, 3):
        pl.semaphore_signal(
            line_sem, inc=1, device_id={"fsdp": peer(d, 0, 0)}, device_id_type=MESH
        )
    g_send(0)
    g_send(1)
    pl.semaphore_wait(line_sem, 3)
    for q in range(2, 5):
        g_send(q)
    b_ring[0][1]()
    for q in range(5, GC):
        g_send(q)

    for load in loads[5:]:
        load.wait()

    def left_root(k, first):
        gk = gq.at[k]
        for n in range(4):
            cols = slice(Q * n, Q * (n + 1))
            term = jnp.dot(ac[k], gk[:, cols], preferred_element_type=F32)
            lg[:, cols] = term if first else lg[:, cols] + term

    def stats(k, first):
        gk = gq.at[k]
        l_o[:, pl.ds(pl.multiple_of(k * Q, Q), Q)] = lax.dot_general(
            gq[r], gk[...], (((1,), (1,)), ((), ())), preferred_element_type=F32
        )
        strip = gk[:, pl.ds(pl.multiple_of(r * Q, Q), Q)]
        for n in range(4):
            cols = slice(Q * n, Q * (n + 1))
            term = lax.dot_general(
                strip, gk[:, cols], (((0,), (0,)), ((), ())), preferred_element_type=F32
            )
            r_o[:, cols] = term if first else r_o[:, cols] + term

    b_ring[1][1]()
    for q in range(GC):
        g_take(q)
        g_ring[q][0]()
        if q >= 2:
            g_ring[q - 2][1]()
    g_ring[GC - 2][1]()
    left_root(r, True)
    g_ring[GC - 1][1]()
    b_ring[2][0]()
    b_ring[3][0]()
    left_root(left, False)
    left_root(right, False)
    own = gq[r].astype(F32)
    part[r, 1] = fold(own * own)
    for q in range(GC):
        g_ring[q][2]()
    left_root(across, False)
    lgb[...] = lg[...].astype(BF16)

    def p_copy(d):
        return pltpu.make_async_remote_copy(
            part.at[r], part.at[r], p_s.at[d - 1], p_r.at[d - 1],
            device_id={"rep": (r + d) % 4}, device_id_type=MESH,
        )

    def product(c):
        b_ring[c][2]()
        p = jnp.dot(lgb[...], bc[c].reshape(BLK, Q), preferred_element_type=F32)
        squares = fold(p * p)
        part[r, 0] = squares if c == 0 else part[r, 0] + squares
        if c == CH - 1:
            for d in (1, 2, 3):
                p_copy(d).start()
        pb = p.astype(BF16)
        for h in range(2):
            rows = slice(128 * h, 128 * (h + 1))
            pieces = jnp.concatenate([pb[rows, 0:128], pb[rows, 128:256]], axis=0)
            out = jnp.dot(perm2[...], pieces, preferred_element_type=F32)
            dsend[c // 2, 32 * h : 32 * (h + 1), c % 2] = out.reshape(32, 8, 128).astype(BF16)

    def d_send(p):
        def body(n, carry):
            to = peer_of(n)
            pltpu.make_async_remote_copy(
                dsend.at[p, to], dret.at[p, f], d_s.at[p], d_r.at[p],
                device_id={"fsdp": to}, device_id_type=MESH,
            ).start()
            return carry

        lax.fori_loop(1, NB, body, 0, unroll=9)
        dret[p, f] = dsend[p, f]

    product(0)
    product(1)
    d_send(0)
    b_ring[2][1]()
    stats(r, True)
    b_ring[3][1]()
    product(2)
    product(3)
    d_send(1)
    for d in (1, 2, 3):
        p_copy(d).wait_recv()
    entries = float(BLK * BLK)
    sums = part[0] + part[1] + part[2] + part[3]
    d_sq = jnp.sum(jnp.sum(sums[0], axis=0, keepdims=True), axis=1, keepdims=True)
    g_sq = jnp.sum(jnp.sum(sums[1], axis=0, keepdims=True), axis=1, keepdims=True)
    scale = jnp.sqrt(g_sq / entries) * lax.rsqrt(d_sq / entries + 1e-06)
    row = jnp.broadcast_to(scale, (1, 128))
    sclsend[...] = row
    scl[f] = row

    def s_start(n, carry):
        pltpu.make_async_remote_copy(
            sclsend, scl.at[f], s_s.at[0], s_r.at[0],
            device_id={"fsdp": peer_of(n)}, device_id_type=MESH,
        ).start()
        return carry

    lax.fori_loop(1, NB, s_start, 0, unroll=9)
    stats(left, False)
    stats(right, False)
    stats(across, False)
    l_o[...] = 0.95 * slbuf[...] + (0.05 / BLK) * l_o[...]
    r_o[...] = 0.95 * srbuf[...] + (0.05 / BLK) * r_o[...]

    pltpu.make_async_remote_copy(
        scl.at[pl.ds(0, NB - 1)], scl.at[pl.ds(0, NB - 1)], s_s.at[0], s_r.at[0],
        device_id={"fsdp": other}, device_id_type=MESH,
    ).wait()
    for p in range(2):
        pltpu.make_async_remote_copy(
            dsend.at[p, pl.ds(0, NB - 1)], dret.at[p, pl.ds(0, NB - 1)], d_s.at[p], d_r.at[p],
            device_id={"fsdp": other}, device_id_type=MESH,
        ).wait()

    def update(b, carry):
        s = own_ref[b]
        step = 0.2 * scl[s]
        for c in range(CH):
            z = zbuf[b, c] - step * dret[c // 2, s, c % 2].astype(F32)
            x = 0.75 * xbuf[b, c] + 0.25 * z
            z_o[b, c] = z
            x_o[b, c] = x
            y_o[b, c] = (0.1 * z + 0.9 * x).astype(BF16)
        return carry

    lax.fori_loop(0, NB, update, 0, unroll=4)

    pltpu.make_async_remote_copy(
        send.at[pl.ds(0, NB - 1)], held.at[pl.ds(0, NB - 1)], g_s.at[0], g_r.at[0],
        device_id={"fsdp": other}, device_id_type=MESH,
    ).wait_send()
    for chunk in b_ring + g_ring:
        chunk[3]()
    for d in (1, 2, 3):
        p_copy(d).wait_send()


def write_kernel(z, x, y, l, r, z_o, x_o, y_o, l_o, r_o, sem):
    copies = [
        pltpu.make_async_copy(a, b, sem.at[n])
        for n, (a, b) in enumerate(((z, z_o), (x, x_o), (y, y_o), (l, l_o), (r, r_o)))
    ]
    for copy in copies:
        copy.start()
    for copy in copies:
        copy.wait()


def pieces_of(flat):
    return flat[0].reshape(4, 512, 128).transpose(1, 0, 2).reshape(NB, CH, 8, 128)


def flat_of(pieces):
    return pieces.reshape(512, 4, 128).transpose(1, 0, 2).reshape(1, 4, 65536)


def per_device(grad, z_params, x_params, owner, stat_left, stat_right, root_left, root_right):
    vmem = pl.BlockSpec(memory_space=pltpu.VMEM)
    anywhere = pl.BlockSpec(memory_space=pl.ANY)
    shapes = (
        ((NB, CH, 8, 128), F32),
        ((NB, CH, 8, 128), F32),
        ((NB, CH, 8, 128), BF16),
        ((Q, BLK), F32),
        ((Q, BLK), F32),
    )
    dma = pltpu.SemaphoreType.DMA
    results = pl.pallas_call(
        remote_kernel,
        out_shape=tuple(pltpu.VMEM(s, t) for s, t in shapes),
        in_specs=[anywhere] * 8,
        out_specs=(vmem,) * 5,
        scratch_shapes=[
            pltpu.VMEM((NB, 32, 128), F32),
            pltpu.VMEM((NB, 32, 128), BF16),
            pltpu.VMEM((NB, 32, 128), BF16),
            pltpu.VMEM((4, Q, BLK), BF16),
            pltpu.VMEM((CH, 4, Q, Q), BF16),
            pltpu.VMEM((4, Q, Q), BF16),
            pltpu.VMEM((Q, BLK), F32),
            pltpu.VMEM((Q, BLK), BF16),
            pltpu.VMEM((NB, CH, 8, 128), F32),
            pltpu.VMEM((NB, CH, 8, 128), F32),
            pltpu.VMEM((Q, BLK), F32),
            pltpu.VMEM((Q, BLK), F32),
            pltpu.VMEM((Q, Q), BF16),
            pltpu.VMEM((Q, Q), BF16),
            pltpu.VMEM((2, NB, 2, 8, 128), BF16),
            pltpu.VMEM((2, NB, 2, 8, 128), BF16),
            pltpu.VMEM((4, 2, 8, 128), F32),
            pltpu.VMEM((NB, 1, 128), F32),
            pltpu.VMEM((1, 128), F32),
            pltpu.VMEM((NB, 128), jnp.int32),
            pltpu.VMEM((1, 128), jnp.int32),
            pltpu.SMEM((1, 128), jnp.int32),
            pltpu.SMEM((NB,), jnp.int32),
            dma((15,)),
            pltpu.SemaphoreType.REGULAR,
            pltpu.SemaphoreType.REGULAR,
            dma((CH + GC, 2)),
            dma((CH + GC, 2)),
            dma((CH + GC, 2)),
            dma((CH + GC, 2)),
            dma((1,)),
            dma((GC,)),
            dma((2,)),
            dma((2,)),
            dma((3,)),
            dma((3,)),
            dma((1,)),
            dma((1,)),
        ],
        compiler_params=pltpu.CompilerParams(
            collective_id=0, has_side_effects=True, vmem_limit_bytes=57 << 20
        ),
        name="shampoo",
    )(
        owner, pieces_of(grad).reshape(NB, 32, 128), pieces_of(z_params), pieces_of(x_params),
        stat_left[0], stat_right[0], root_left[0], root_right[0],
    )
    z, x, y, left_new, right_new = pl.pallas_call(
        write_kernel,
        out_shape=tuple(jax.ShapeDtypeStruct(s, t) for s, t in shapes),
        in_specs=[vmem] * 5,
        out_specs=(anywhere,) * 5,
        scratch_shapes=[dma((5,))],
        compiler_params=pltpu.CompilerParams(vmem_limit_bytes=8 << 20),
        name="write",
    )(*results)
    return (flat_of(z), flat_of(x), flat_of(y), left_new[None], right_new[None])


def solution(mesh):
    return jax.shard_map(
        per_device,
        mesh=mesh,
        in_specs=(P("rep", "fsdp", None),) * 3 + (P(),) + (P("fsdp", "rep", None),) * 4,
        out_specs=(P("rep", "fsdp", None),) * 3 + (P("fsdp", "rep", None),) * 2,
        check_vma=False,
    )
```
